32 devices in a mesh: seq: 8 (over z, y), head: 4 (over x, core).
Axes of the slice: x: 2, y: 2, z: 4, core: 2. Of those that a mesh axis runs over, the one named last changes fastest.
Arguments:
- query: bfloat16 [384, 1536], P('seq', 'head'), may hold values from -64 to 64
- new_kv: bfloat16 [2, 384, 1536], P(None, 'seq', 'head'), may hold values from -6 to 6
- cache_kv: bfloat16 [2, 1024, 1536], P(None, 'seq', 'head'), may hold values from -6 to 6
- text_kv: bfloat16 [2, 512, 1536], P(None, None, 'head'), may hold values from -8 to 8
- active: int32 [384], P('seq'), may hold values from 0 to 1023, as said below
- counts: int32 [8], P('seq'), may hold values from 0 to 48, as said below
- hidden: bfloat16 [384, 3072], P('seq', 'head'), may hold values from -64 to 64
- w_out: bfloat16 [1536, 3072], P('head'), may hold values from -0.4375 to 0.4375
- mod_shift: float32 [3072], P('head'), may hold values from -3 to 3
- mod_scale: float32 [3072], P('head'), may hold values from -3 to 3
- w_final: float32 [3072, 64], P('head'), may hold values from -0.109375 to 0.109375
- latent: float32 [1024, 64], P('seq'), may hold values from -6 to 6
- cached_velocity: float32 [1024, 64], P('seq'), may hold values from -6 to 6
- step_size: float32 [1], replicated, may hold values from -0.6 to -0.1
Outputs:
- velocity: float32 [1024, 64], P('seq')
- latent_next: float32 [1024, 64], P('seq')
The draws below stay inside these ranges and needn't reach their ends.
Inputs may be any that keep to these rules, and one draw needn't show every extreme that they name: `active`: for shard k, the entries k * 48 to k * 48 + counts[k] - 1 are distinct image tokens of that shard (k * 128 to (k + 1) * 128 - 1); the later entries of the shard are tokens of the same shard and carry no meaning. The counts sum to exactly 24 times the number of shards; some shard has 48 and some shard has 0.
All inputs are finite; a program needn't handle non-finite values.
Results may differ from the reference program's by a relative error of at most 0.0035.
Values may be sent and summed in bfloat16 or wider, within the bound.
A program may use at most 128 MiB of HBM per device.

```python
import math
import jax
import jax.numpy as jnp
from jax import lax

D = 3072
HEADS = 12
HD = 128
CH = 64
TEXT = 512
TOK_DEV = 128
ACT_DEV = 24
CAP = 48
TOKENS = 1024
SLOTS = 384
HW = 1536
N_SEQ = 8


def active_plan(key):
    root_key = jax.random.fold_in(key, 11)
    shards = TOKENS // TOK_DEV
    ordering = jax.random.permutation(jax.random.fold_in(root_key, 1), shards)
    margin = CAP - ACT_DEV
    uplift = jax.random.randint(jax.random.fold_in(root_key, 2), (shards // 2,), 0, margin + 1)
    uplift = uplift.at[0].set(margin)
    counts = jnp.zeros((shards,), jnp.int32)
    counts = counts.at[ordering[0::2]].set(ACT_DEV + uplift)
    counts = counts.at[ordering[1::2]].set(ACT_DEV - uplift)
    pick_keys = jax.random.split(jax.random.fold_in(root_key, 3), shards)
    within = jax.vmap(lambda pick_key: jax.random.permutation(pick_key, TOK_DEV)[:CAP])(pick_keys)
    offsets = (jnp.arange(shards) * TOK_DEV)[:, None]
    return (counts.astype(jnp.int32), (within + offsets).reshape(-1).astype(jnp.int32))


def draw_active(key, part):
    return active_plan(key)[1]


def draw_counts(key, part):
    return active_plan(key)[0]


def attention_inputs(key):
    root_key = jax.random.fold_in(key, 23)
    queries = 2.5 * jax.random.truncated_normal(jax.random.fold_in(root_key, 1), -4.0, 4.0, (SLOTS, HW), jnp.float32)
    text_rows = jax.random.truncated_normal(jax.random.fold_in(root_key, 2), -4.0, 4.0, (2, TEXT, HW), jnp.float32)
    text_rows = text_rows.at[0].multiply(1.25)
    return (queries, text_rows)


def draw_query(key, part):
    return attention_inputs(key)[0].astype(jnp.bfloat16)


def draw_text_kv(key, part):
    return attention_inputs(key)[1].astype(jnp.bfloat16)


def draw_hidden(key, part):
    root_key = jax.random.fold_in(key, 31)
    col_log = jnp.arange(D, dtype=jnp.float32) / D * math.log(3.0) + jax.random.uniform(jax.random.fold_in(root_key, 1), (D,), jnp.float32, 0.0, math.log(10.0 / 3.0))
    row_log = jax.random.uniform(jax.random.fold_in(root_key, 2), (SLOTS, 1), jnp.float32, 0.0, math.log(10.0))
    noise = jax.random.truncated_normal(jax.random.fold_in(root_key, 3), -4.0, 4.0, (SLOTS, D), jnp.float32)
    return (0.1 * jnp.exp(row_log) * jnp.exp(col_log)[None, :] * noise).astype(jnp.bfloat16)


def level_of(stream_key, dims, cuts, least, high):
    loudness, own = 1.0, jax.random.fold_in(stream_key, 6)
    for dim, parts in cuts:
        steps = jnp.exp(jax.random.uniform(jax.random.fold_in(own, dim), (parts,), jnp.float32, least / len(cuts), high / len(cuts)))
        loudness = loudness * jnp.repeat(steps, dims[dim] // parts).reshape([-1 if axis == dim else 1 for axis in range(len(dims))])
    return loudness


def gaussian(stream_key, extent, scale, bound, cuts=(), kind=jnp.bfloat16):
    factor_of = level_of(stream_key, extent, cuts, -0.22, 0.18) if cuts else 1.0
    values = jax.random.normal(stream_key, extent, jnp.float32) * scale * factor_of
    return jnp.minimum(jnp.maximum(values, -bound), bound).astype(kind)


def setup_inputs(seed: int = 0) -> dict:
    seeds = jax.random.split(jax.random.key(seed), 15)
    return {
        "query": draw_query(jax.random.fold_in(seeds[14], 71), 0),
        "new_kv": gaussian(seeds[1], (2, SLOTS, HW), 1.0, 6.0, ((1, 8), (2, 4))),
        "cache_kv": gaussian(seeds[2], (2, TOKENS, HW), 1.0, 6.0, ((1, 8), (2, 4))),
        "text_kv": draw_text_kv(jax.random.fold_in(seeds[14], 71), 0),
        "active": draw_active(jax.random.fold_in(seeds[14], 71), 0),
        "counts": draw_counts(jax.random.fold_in(seeds[14], 71), 0),
        "hidden": draw_hidden(jax.random.fold_in(seeds[14], 71), 0),
        "w_out": gaussian(seeds[7], (HW, D), (HW // 8) ** -0.5, 0.4375, ((0, 4),)),
        "mod_shift": gaussian(seeds[8], (D,), 0.5, 3.0, ((0, 4),), jnp.float32),
        "mod_scale": gaussian(seeds[9], (D,), 0.5, 3.0, ((0, 4),), jnp.float32),
        "w_final": gaussian(seeds[10], (D, CH), D ** -0.5, 0.109375, ((0, 4),), jnp.float32),
        "latent": gaussian(seeds[11], (TOKENS, CH), 1.0, 6.0, ((0, 8),), jnp.float32),
        "cached_velocity": gaussian(seeds[12], (TOKENS, CH), 1.0, 6.0, ((0, 8),), jnp.float32),
        "step_size": jnp.clip(jax.random.uniform(seeds[13], (1,), jnp.float32, -0.6, -0.1), -0.6, -0.1),
    }


EPS = 1e-06

def reference(query, new_kv, cache_kv, text_kv, active, counts, hidden, w_out, mod_shift, mod_scale, w_final, latent, cached_velocity, step_size):
    slot_ids = jnp.arange(CAP * N_SEQ, dtype=jnp.int32)
    live_slots = slot_ids % CAP < counts[slot_ids // CAP]
    target = jnp.where(live_slots, active, TOKENS).astype(jnp.int32)
    image_kv = cache_kv.at[:, target].set(new_kv, mode='drop')
    all_keys = jnp.concatenate([image_kv[0], text_kv[0]], axis=0).astype(jnp.float32)
    all_values = jnp.concatenate([image_kv[1], text_kv[1]], axis=0).astype(jnp.float32)
    key_count = all_keys.shape[0]
    keys_split = all_keys.reshape(key_count, HEADS, HD)
    values_split = all_values.reshape(key_count, HEADS, HD)
    score_scale = HD ** (-0.5)

    def one_block(queries):
        split = queries.astype(jnp.float32).reshape(CAP, HEADS, HD)
        scores = jnp.einsum('qhd,khd->hqk', split, keys_split) * score_scale
        row_max = lax.optimization_barrier(jnp.max(scores, axis=2, keepdims=True))
        weights = jnp.exp(scores - row_max)
        weight_sum = lax.optimization_barrier(jnp.sum(weights, axis=2))
        rounded = lax.optimization_barrier(weights.astype(jnp.bfloat16)).astype(jnp.float32)
        numerator = jnp.einsum('hqk,khd->qhd', rounded, values_split)
        return (numerator / jnp.transpose(weight_sum)[:, :, None]).reshape(CAP, HW).astype(jnp.bfloat16)
    attended = lax.map(one_block, query.reshape(N_SEQ, CAP, HW)).reshape(CAP * N_SEQ, HW)
    projected = jnp.dot(attended, w_out, preferred_element_type=jnp.float32)
    residual_sum = hidden.astype(jnp.float32) + projected
    row_mean = lax.optimization_barrier(jnp.mean(residual_sum, axis=1, keepdims=True))
    row_var = lax.optimization_barrier(jnp.mean(jnp.square(residual_sum - row_mean), axis=1, keepdims=True))
    normed = (residual_sum - row_mean) / jnp.sqrt(row_var + EPS) * (1.0 + mod_scale) + mod_shift
    fresh = jnp.dot(normed, w_final, precision=lax.Precision.HIGHEST)
    velocity = cached_velocity.at[target].set(fresh, mode='drop')
    latent_next = latent + step_size[0] * velocity
    return (velocity, latent_next)
```

```python
import functools

import jax
import jax.numpy as jnp
from jax import lax
from jax.experimental import pallas as pl
from jax.experimental.pallas import tpu as pltpu
from jax.sharding import PartitionSpec as P

HD = 128
EPS = 1e-06
MESH = pl.DeviceIdType.MESH
HIGH = lax.Precision.HIGHEST


def loop(first, last, body, carry):
    if last - first <= 8:
        for d in range(first, last):
            carry = body(d, carry)
        return carry
    return lax.fori_loop(first, last, body, carry)


def kernel(
    n_seq,
    n_head,
    pair,
    query,
    new_kv,
    cache_kv,
    text_hbm,
    active,
    counts,
    hidden,
    w_out_hbm,
    mod_shift,
    mod_scale,
    w_final,
    latent,
    cached_velocity,
    step_size,
    velocity,
    latent_next,
    q_all,
    kv,
    text,
    w_out,
    part_send,
    part_recv,
    stat_send,
    stat_recv,
    cols_send,
    cols_recv,
    sums,
    local_sem,
    kv_send_sem,
    kv_recv_sem,
    q_send_sem,
    q_recv_sem,
    part_send_sem,
    part_recv_sem,
    stat_send_sem,
    stat_recv_sem,
    cols_send_sem,
    cols_recv_sem,
    sums_send_sem,
    sums_recv_sem,
):
    seq = lax.axis_index("seq")
    head = lax.axis_index("head")
    slots, width = query.shape
    tokens = cache_kv.shape[1]
    heads = width // HD
    groups = n_seq // pair
    group = seq // pair
    place = seq % pair
    model = n_head * hidden.shape[1]
    share = hidden.shape[1]
    channels = w_final.shape[1]

    def group_peer(d):
        return lax.rem(group + d, groups)

    def head_peer(d):
        return lax.rem(head + d, n_head)

    barrier = pltpu.get_barrier_semaphore()

    def greet(d, carry):
        pl.semaphore_signal(
            barrier, inc=1, device_id=(group_peer(d) * pair + place, head), device_id_type=MESH
        )
        return carry

    loop(1, groups, greet, 0)
    partner = group * pair + (pair - 1 - place)
    if pair == 2:
        pl.semaphore_signal(barrier, inc=1, device_id=(partner, head), device_id_type=MESH)
    for d in range(1, n_head):
        pl.semaphore_signal(barrier, inc=1, device_id=(seq, head_peer(d)), device_id_type=MESH)

    local = [pltpu.make_async_copy(text_hbm, text, local_sem.at[0])]
    for d in range(n_head):
        at = pl.ds(pl.multiple_of(head_peer(d) * share, 128), share)
        local.append(
            pltpu.make_async_copy(w_out_hbm.at[:, at], w_out.at[d], local_sem.at[1 + d])
        )
    for copy in local:
        copy.start()

    positions = active[...] - seq * tokens
    slot_ids = lax.broadcasted_iota(jnp.int32, (1, slots), 1)
    positions = jnp.where(slot_ids < counts[0], positions, -1)
    matched = lax.broadcasted_iota(jnp.int32, (tokens, slots), 0) == positions
    one_hot = matched.astype(jnp.float32)
    replaced = jnp.max(one_hot, axis=1, keepdims=True) > 0.5

    def place_rows(which):
        placed = jnp.dot(
            one_hot.astype(jnp.bfloat16), new_kv[which], preferred_element_type=jnp.float32
        )
        own = cache_kv[which].astype(jnp.float32)
        kv[which, 0] = jnp.where(replaced, placed, own).astype(jnp.bfloat16)

    place_rows(0)
    place_rows(1)

    pl.semaphore_wait(barrier, groups - 1 + pair - 1 + n_head - 1)

    def q_copy(d):
        return pltpu.make_async_remote_copy(
            src_ref=query,
            dst_ref=q_all.at[group],
            send_sem=q_send_sem.at[d],
            recv_sem=q_recv_sem.at[group],
            device_id=(group_peer(d) * pair + place, head),
            device_id_type=MESH,
        )

    def kv_copy(which):
        return pltpu.make_async_remote_copy(
            src_ref=kv.at[which, 0],
            dst_ref=kv.at[which, 1],
            send_sem=kv_send_sem.at[which],
            recv_sem=kv_recv_sem.at[which],
            device_id=(partner, head),
            device_id_type=MESH,
        )

    def start_q(d, carry):
        q_copy(d).start()
        return carry

    if pair == 2:
        kv_copy(0).start()
    loop(1, groups, start_q, 0)
    if pair == 2:
        kv_copy(1).start()

    def attend(rows, keys, values):
        result = []
        for h in range(heads):
            at = slice(h * HD, (h + 1) * HD)
            scores = lax.dot_general(
                rows[:, at],
                keys[:, at],
                (((1,), (1,)), ((), ())),
                preferred_element_type=jnp.float32,
            ) * HD ** (-0.5)
            top = jnp.max(scores, axis=1, keepdims=True)
            weights = jnp.exp(scores - top)
            total = jnp.sum(weights, axis=1, keepdims=True)
            blend = jnp.dot(
                weights.astype(jnp.bfloat16), values[:, at], preferred_element_type=jnp.float32
            )
            result.append((blend, top, total))
        return result

    def merge(first, second):
        result = []
        for (blend_a, top_a, total_a), (blend_b, top_b, total_b) in zip(first, second):
            top = jnp.maximum(top_a, top_b)
            share_a, share_b = jnp.exp(top_a - top), jnp.exp(top_b - top)
            result.append(
                (
                    blend_a * share_a + blend_b * share_b,
                    top,
                    total_a * share_a + total_b * share_b,
                )
            )
        return result

    lifted = 1.0 + mod_scale[...]
    rows8 = lax.broadcasted_iota(jnp.int32, (8, share), 0)
    pairs = jnp.where(rows8 == 0, lifted, jnp.where(rows8 == 1, mod_shift[...], 0.0))
    sums[head, slots : slots + 8, 0:channels] = jnp.dot(
        pairs, w_final[...], precision=HIGH, preferred_element_type=jnp.float32
    )
    local[0].wait()
    state = attend(query[...], text[0], text[1])

    if pair == 2:
        kv_copy(0).wait_recv()
        kv_copy(1).wait_recv()
    keys = kv[0].reshape(pair * tokens, width)
    values = kv[1].reshape(pair * tokens, width)

    def part_copy(d):
        return pltpu.make_async_remote_copy(
            src_ref=part_send.at[d],
            dst_ref=part_recv.at[group],
            send_sem=part_send_sem.at[d],
            recv_sem=part_recv_sem.at[group],
            device_id=(group_peer(d) * pair + place, head),
            device_id_type=MESH,
        )

    def stat_copy(d):
        return pltpu.make_async_remote_copy(
            src_ref=stat_send.at[d],
            dst_ref=stat_recv.at[group],
            send_sem=stat_send_sem.at[d],
            recv_sem=stat_recv_sem.at[group],
            device_id=(group_peer(d) * pair + place, head),
            device_id_type=MESH,
        )

    def arrived(buffer, sems, source):
        pltpu.make_async_remote_copy(
            src_ref=buffer.at[source],
            dst_ref=buffer.at[source],
            send_sem=q_send_sem.at[0],
            recv_sem=sems.at[source],
            device_id=(source * pair + place, head),
            device_id_type=MESH,
        ).wait_recv()

    lanes = lax.broadcasted_iota(jnp.int32, (slots, HD), 1)

    def answer(d, carry):
        source = group_peer(d)
        arrived(q_all, q_recv_sem, source)
        spread = jnp.zeros((slots, HD), jnp.float32)
        for h, (blend, top, total) in enumerate(attend(q_all[source], keys, values)):
            part_send[d, :, h * HD : (h + 1) * HD] = (blend / total).astype(jnp.bfloat16)
            spread = jnp.where(lanes == h, top + jnp.log(total), spread)
        stat_send[d] = jnp.transpose(spread)[:8]
        stat_copy(d).start()
        part_copy(d).start()
        return carry

    loop(1, groups, answer, 0)
    state = merge(state, attend(query[...], keys, values))

    def gather(d, carry):
        source = lax.rem(group + groups - d, groups)
        arrived(stat_recv, stat_recv_sem, source)
        arrived(part_recv, part_recv_sem, source)
        spread = jnp.transpose(stat_recv[source])
        other = [
            (
                part_recv[source, :, h * HD : (h + 1) * HD].astype(jnp.float32),
                spread[:, h : h + 1],
                jnp.ones((slots, 1), jnp.float32),
            )
            for h in range(heads)
        ]
        return merge(carry, other)

    state = loop(1, groups, gather, state)
    attended = jnp.concatenate(
        [(blend / total).astype(jnp.bfloat16) for blend, top, total in state], axis=1
    )

    def cols_copy(d):
        return pltpu.make_async_remote_copy(
            src_ref=cols_send.at[d],
            dst_ref=cols_recv.at[d],
            send_sem=cols_send_sem.at[d],
            recv_sem=cols_recv_sem.at[d],
            device_id=(seq, head_peer(d)),
            device_id_type=MESH,
        )

    for d in range(1, n_head):
        local[1 + d].wait()
        cols_send[d] = jnp.dot(attended, w_out[d], preferred_element_type=jnp.float32).astype(
            jnp.bfloat16
        )
        cols_copy(d).start()
    local[1].wait()
    residual = hidden[...].astype(jnp.float32) + jnp.dot(
        attended, w_out[0], preferred_element_type=jnp.float32
    )
    for d in range(1, n_head):
        cols_copy(d).wait_recv()
        residual = residual + cols_recv[d].astype(jnp.float32)

    mean_here = jnp.sum(residual, axis=1, keepdims=True) / share
    centred = residual - mean_here
    square_here = jnp.sum(centred * centred, axis=1, keepdims=True)
    scaled = jnp.dot(
        centred * lifted, w_final[...], precision=HIGH, preferred_element_type=jnp.float32
    )
    sums[head, 0:slots, 0:channels] = scaled
    sums[head, 0:slots, channels : channels + 1] = mean_here
    sums[head, 0:slots, channels + 1 : channels + 2] = square_here

    def sums_copy(d):
        return pltpu.make_async_remote_copy(
            src_ref=sums.at[head],
            dst_ref=sums.at[head],
            send_sem=sums_send_sem.at[d],
            recv_sem=sums_recv_sem.at[head],
            device_id=(seq, head_peer(d)),
            device_id_type=MESH,
        )

    for d in range(1, n_head):
        sums_copy(d).start()
    for d in range(1, n_head):
        source = head_peer(d)
        pltpu.make_async_remote_copy(
            src_ref=sums.at[source],
            dst_ref=sums.at[source],
            send_sem=sums_send_sem.at[0],
            recv_sem=sums_recv_sem.at[source],
            device_id=(seq, source),
            device_id_type=MESH,
        ).wait_recv()

    means = [sums[i, 0:slots, channels : channels + 1] for i in range(n_head)]
    mean = sum(means[1:], means[0]) / n_head
    squares = jnp.zeros((slots, 1), jnp.float32)
    fresh = jnp.zeros((slots, channels), jnp.float32)
    offset = jnp.zeros((1, channels), jnp.float32)
    for i in range(n_head):
        away = means[i] - mean
        squares = squares + sums[i, 0:slots, channels + 1 : channels + 2] + share * away * away
        column = sums[i, slots : slots + 1, 0:channels]
        fresh = fresh + sums[i, 0:slots, 0:channels] + away * column
        offset = offset + sums[i, slots + 1 : slots + 2, 0:channels]
    fresh = fresh * lax.rsqrt(squares / model + EPS) + offset
    chosen = jnp.dot(one_hot, fresh, precision=HIGH, preferred_element_type=jnp.float32)
    refreshed = jnp.where(replaced, chosen, cached_velocity[...])
    velocity[...] = refreshed
    latent_next[...] = latent[...] + step_size[0] * refreshed

    if pair == 2:
        kv_copy(0).wait_send()
        kv_copy(1).wait_send()

    def drain(d, carry):
        q_copy(d).wait_send()
        part_copy(d).wait_send()
        stat_copy(d).wait_send()
        return carry

    loop(1, groups, drain, 0)
    for d in range(1, n_head):
        cols_copy(d).wait_send()
        sums_copy(d).wait_send()


def on_device(
    n_seq,
    n_head,
    query,
    new_kv,
    cache_kv,
    text_kv,
    active,
    counts,
    hidden,
    w_out,
    mod_shift,
    mod_scale,
    w_final,
    latent,
    cached_velocity,
    step_size,
):
    slots, width = query.shape
    tokens = cache_kv.shape[1]
    share = hidden.shape[1]
    channels = w_final.shape[1]
    pair = 2 if n_seq % 2 == 0 else 1
    groups = n_seq // pair
    vmem = pl.BlockSpec(memory_space=pltpu.VMEM)
    smem = pl.BlockSpec(memory_space=pltpu.SMEM)
    hbm = pl.BlockSpec(memory_space=pl.ANY)
    dma = pltpu.SemaphoreType.DMA
    flops = 2 * slots * (2 * width * (n_seq * tokens + text_kv.shape[1]) + width * share * n_head)
    return pl.pallas_call(
        functools.partial(kernel, n_seq, n_head, pair),
        out_shape=(
            jax.ShapeDtypeStruct(latent.shape, jnp.float32),
            jax.ShapeDtypeStruct(latent.shape, jnp.float32),
        ),
        in_specs=[
            vmem,
            vmem,
            vmem,
            hbm,
            vmem,
            smem,
            vmem,
            hbm,
            vmem,
            vmem,
            vmem,
            vmem,
            vmem,
            smem,
        ],
        out_specs=(vmem, vmem),
        scratch_shapes=[
            pltpu.VMEM((groups, slots, width), jnp.bfloat16),
            pltpu.VMEM((2, pair, tokens, width), jnp.bfloat16),
            pltpu.VMEM(text_kv.shape, jnp.bfloat16),
            pltpu.VMEM((n_head, width, share), jnp.bfloat16),
            pltpu.VMEM((groups, slots, width), jnp.bfloat16),
            pltpu.VMEM((groups, slots, width), jnp.bfloat16),
            pltpu.VMEM((groups, 8, slots), jnp.float32),
            pltpu.VMEM((groups, 8, slots), jnp.float32),
            pltpu.VMEM((n_head, slots, share), jnp.bfloat16),
            pltpu.VMEM((n_head, slots, share), jnp.bfloat16),
            pltpu.VMEM((n_head, slots + 8, 128), jnp.float32),
            dma((1 + n_head,)),
            dma((2,)),
            dma((2,)),
            dma((groups,)),
            dma((groups,)),
            dma((groups,)),
            dma((groups,)),
            dma((groups,)),
            dma((groups,)),
            dma((n_head,)),
            dma((n_head,)),
            dma((n_head,)),
            dma((n_head,)),
        ],
        compiler_params=pltpu.CompilerParams(
            collective_id=0, has_side_effects=True, vmem_limit_bytes=40 * 1024 * 1024
        ),
        cost_estimate=pl.CostEstimate(
            flops=flops, bytes_accessed=2 * w_out.size, transcendentals=0
        ),
    )(
        query,
        new_kv,
        cache_kv,
        text_kv,
        active.reshape(1, slots),
        counts,
        hidden,
        w_out,
        mod_shift.reshape(1, share),
        mod_scale.reshape(1, share),
        w_final,
        latent,
        cached_velocity,
        step_size,
    )


def solution(mesh):
    in_specs = (
        P("seq", "head"),
        P(None, "seq", "head"),
        P(None, "seq", "head"),
        P(None, None, "head"),
        P("seq"),
        P("seq"),
        P("seq", "head"),
        P("head", None),
        P("head"),
        P("head"),
        P("head", None),
        P("seq", None),
        P("seq", None),
        P(),
    )
    out_specs = (P("seq", None), P("seq", None))
    return jax.shard_map(
        functools.partial(on_device, mesh.shape["seq"], mesh.shape["head"]),
        mesh=mesh,
        in_specs=in_specs,
        out_specs=out_specs,
        check_vma=False,
    )
```

```python
import functools

import jax
import jax.numpy as jnp
from jax import lax
from jax.experimental import pallas as pl
from jax.experimental.pallas import tpu as pltpu
from jax.sharding import PartitionSpec as P

HD = 128
EPS = 1e-06
MESH = pl.DeviceIdType.MESH
HIGH = lax.Precision.HIGHEST


def loop(first, last, body, carry):
    if last - first <= 8:
        for d in range(first, last):
            carry = body(d, carry)
        return carry
    return lax.fori_loop(first, last, body, carry)


def kernel(
    n_seq,
    n_head,
    pair,
    query_hbm,
    new_kv_hbm,
    cache_kv_hbm,
    text_hbm,
    active_hbm,
    counts_hbm,
    hidden_hbm,
    w_out_hbm,
    mod_shift_hbm,
    mod_scale_hbm,
    w_final_hbm,
    chosen,
    renewed,
    query,
    new_kv,
    cache_kv,
    active,
    counts,
    hidden,
    mod_shift,
    mod_scale,
    w_final,
    q_all,
    kv,
    text,
    w_out,
    part_send,
    part_recv,
    stat_send,
    stat_recv,
    cols_send,
    cols_recv,
    sums,
    local_sem,
    kv_send_sem,
    kv_recv_sem,
    q_send_sem,
    q_recv_sem,
    part_send_sem,
    part_recv_sem,
    stat_send_sem,
    stat_recv_sem,
    cols_send_sem,
    cols_recv_sem,
    sums_send_sem,
    sums_recv_sem,
):
    seq = lax.axis_index("seq")
    head = lax.axis_index("head")
    slots, width = query.shape
    tokens = cache_kv.shape[1]
    heads = width // HD
    groups = n_seq // pair
    group = seq // pair
    place = seq % pair
    model = n_head * hidden.shape[1]
    share = hidden.shape[1]
    channels = w_final.shape[0]

    def group_peer(d):
        return lax.rem(group + d, groups)

    def head_peer(d):
        return lax.rem(head + d, n_head)

    barrier = pltpu.get_barrier_semaphore()

    def greet(d, carry):
        pl.semaphore_signal(
            barrier, inc=1, device_id=(group_peer(d) * pair + place, head), device_id_type=MESH
        )
        return carry

    loop(1, groups, greet, 0)
    partner = group * pair + (pair - 1 - place)
    if pair == 2:
        pl.semaphore_signal(barrier, inc=1, device_id=(partner, head), device_id_type=MESH)
    for d in range(1, n_head):
        pl.semaphore_signal(barrier, inc=1, device_id=(seq, head_peer(d)), device_id_type=MESH)

    local = []

    def fetch(source, target):
        copy = pltpu.make_async_copy(source, target, local_sem.at[len(local)])
        copy.start()
        local.append(copy)
        return copy

    first_in = [
        fetch(query_hbm, query),
        fetch(active_hbm, active),
        fetch(counts_hbm, counts),
        fetch(new_kv_hbm, new_kv),
        fetch(cache_kv_hbm, cache_kv),
    ]
    text_in = fetch(text_hbm, text)
    norm_in = [
        fetch(mod_shift_hbm, mod_shift),
        fetch(mod_scale_hbm, mod_scale),
        fetch(w_final_hbm, w_final),
    ]
    w_out_in = [None] * n_head
    for d in [*range(1, n_head), 0]:
        at = pl.ds(pl.multiple_of(head_peer(d) * share, 128), share)
        w_out_in[d] = fetch(w_out_hbm.at[:, at], w_out.at[d])
    hidden_in = fetch(hidden_hbm, hidden)
    for copy in first_in:
        copy.wait()

    positions = active[...] - seq * tokens
    slot_ids = lax.broadcasted_iota(jnp.int32, (1, slots), 1)
    positions = jnp.where(slot_ids < counts[0], positions, -1)
    matched = lax.broadcasted_iota(jnp.int32, (tokens, slots), 0) == positions
    one_hot = matched.astype(jnp.float32)
    replaced = jnp.max(one_hot, axis=1, keepdims=True) > 0.5

    def place_rows(which):
        placed = jnp.dot(
            one_hot.astype(jnp.bfloat16), new_kv[which], preferred_element_type=jnp.float32
        )
        own = cache_kv[which].astype(jnp.float32)
        kv[which, 0] = jnp.where(replaced, placed, own).astype(jnp.bfloat16)

    place_rows(0)
    place_rows(1)
    renewed[...] = jnp.transpose(
        jnp.broadcast_to(replaced.astype(jnp.float32), (tokens, channels))
    )

    pl.semaphore_wait(barrier, groups - 1 + pair - 1 + n_head - 1)

    def q_copy(d):
        return pltpu.make_async_remote_copy(
            src_ref=query,
            dst_ref=q_all.at[group],
            send_sem=q_send_sem.at[d],
            recv_sem=q_recv_sem.at[group],
            device_id=(group_peer(d) * pair + place, head),
            device_id_type=MESH,
        )

    def kv_copy(which):
        return pltpu.make_async_remote_copy(
            src_ref=kv.at[which, 0],
            dst_ref=kv.at[which, 1],
            send_sem=kv_send_sem.at[which],
            recv_sem=kv_recv_sem.at[which],
            device_id=(partner, head),
            device_id_type=MESH,
        )

    def start_q(d, carry):
        q_copy(d).start()
        return carry

    if pair == 2:
        kv_copy(0).start()
    loop(1, groups, start_q, 0)
    if pair == 2:
        kv_copy(1).start()

    def attend(rows, keys, values):
        result = []
        for h in range(heads):
            at = slice(h * HD, (h + 1) * HD)
            scores = lax.dot_general(
                rows[:, at],
                keys[:, at],
                (((1,), (1,)), ((), ())),
                preferred_element_type=jnp.float32,
            ) * HD ** (-0.5)
            top = jnp.max(scores, axis=1, keepdims=True)
            weights = jnp.exp(scores - top)
            total = jnp.sum(weights, axis=1, keepdims=True)
            blend = jnp.dot(
                weights.astype(jnp.bfloat16), values[:, at], preferred_element_type=jnp.float32
            )
            result.append((blend, top, total))
        return result

    def merge(first, second):
        result = []
        for (blend_a, top_a, total_a), (blend_b, top_b, total_b) in zip(first, second):
            top = jnp.maximum(top_a, top_b)
            share_a, share_b = jnp.exp(top_a - top), jnp.exp(top_b - top)
            result.append(
                (
                    blend_a * share_a + blend_b * share_b,
                    top,
                    total_a * share_a + total_b * share_b,
                )
            )
        return result

    for copy in norm_in:
        copy.wait()

    def as_row(ref):
        return jnp.concatenate([ref[i : i + 1, :] for i in range(ref.shape[0])], axis=1)

    lifted = 1.0 + as_row(mod_scale)

    def final_dot(rows):
        return lax.dot_general(
            rows,
            w_final[...],
            (((1,), (1,)), ((), ())),
            precision=HIGH,
            preferred_element_type=jnp.float32,
        )

    rows8 = lax.broadcasted_iota(jnp.int32, (8, share), 0)
    pairs = jnp.where(rows8 == 0, lifted, jnp.where(rows8 == 1, as_row(mod_shift), 0.0))
    sums[head, slots : slots + 8, 0:channels] = final_dot(pairs)
    text_in.wait()
    state = attend(query[...], text[0], text[1])

    if pair == 2:
        kv_copy(0).wait_recv()
        kv_copy(1).wait_recv()
    keys = kv[0].reshape(pair * tokens, width)
    values = kv[1].reshape(pair * tokens, width)

    def part_copy(d):
        return pltpu.make_async_remote_copy(
            src_ref=part_send.at[d],
            dst_ref=part_recv.at[group],
            send_sem=part_send_sem.at[d],
            recv_sem=part_recv_sem.at[group],
            device_id=(group_peer(d) * pair + place, head),
            device_id_type=MESH,
        )

    def stat_copy(d):
        return pltpu.make_async_remote_copy(
            src_ref=stat_send.at[d],
            dst_ref=stat_recv.at[group],
            send_sem=stat_send_sem.at[d],
            recv_sem=stat_recv_sem.at[group],
            device_id=(group_peer(d) * pair + place, head),
            device_id_type=MESH,
        )

    def arrived(buffer, sems, source):
        pltpu.make_async_remote_copy(
            src_ref=buffer.at[source],
            dst_ref=buffer.at[source],
            send_sem=q_send_sem.at[0],
            recv_sem=sems.at[source],
            device_id=(source * pair + place, head),
            device_id_type=MESH,
        ).wait_recv()

    lanes = lax.broadcasted_iota(jnp.int32, (slots, HD), 1)

    def answer(d, carry):
        source = group_peer(d)
        arrived(q_all, q_recv_sem, source)
        spread = jnp.zeros((slots, HD), jnp.float32)
        for h, (blend, top, total) in enumerate(attend(q_all[source], keys, values)):
            part_send[d, :, h * HD : (h + 1) * HD] = (blend / total).astype(jnp.bfloat16)
            spread = jnp.where(lanes == h, top + jnp.log(total), spread)
        stat_send[d] = jnp.transpose(spread)[:8]
        stat_copy(d).start()
        part_copy(d).start()
        return carry

    loop(1, groups, answer, 0)
    state = merge(state, attend(query[...], keys, values))

    def gather(d, carry):
        source = lax.rem(group + groups - d, groups)
        arrived(stat_recv, stat_recv_sem, source)
        arrived(part_recv, part_recv_sem, source)
        spread = jnp.transpose(stat_recv[source])
        other = [
            (
                part_recv[source, :, h * HD : (h + 1) * HD].astype(jnp.float32),
                spread[:, h : h + 1],
                jnp.ones((slots, 1), jnp.float32),
            )
            for h in range(heads)
        ]
        return merge(carry, other)

    state = loop(1, groups, gather, state)
    attended = jnp.concatenate(
        [(blend / total).astype(jnp.bfloat16) for blend, top, total in state], axis=1
    )

    def cols_copy(d):
        return pltpu.make_async_remote_copy(
            src_ref=cols_send.at[d],
            dst_ref=cols_recv.at[d],
            send_sem=cols_send_sem.at[d],
            recv_sem=cols_recv_sem.at[d],
            device_id=(seq, head_peer(d)),
            device_id_type=MESH,
        )

    for d in range(1, n_head):
        w_out_in[d].wait()
        cols_send[d] = jnp.dot(attended, w_out[d], preferred_element_type=jnp.float32).astype(
            jnp.bfloat16
        )
        cols_copy(d).start()
    w_out_in[0].wait()
    hidden_in.wait()
    residual = hidden[...].astype(jnp.float32) + jnp.dot(
        attended, w_out[0], preferred_element_type=jnp.float32
    )
    for d in range(1, n_head):
        cols_copy(d).wait_recv()
        residual = residual + cols_recv[d].astype(jnp.float32)

    mean_here = jnp.sum(residual, axis=1, keepdims=True) / share
    centred = residual - mean_here
    square_here = jnp.sum(centred * centred, axis=1, keepdims=True)
    scaled = final_dot(centred * lifted)
    sums[head, 0:slots, 0:channels] = scaled
    sums[head, 0:slots, channels : channels + 1] = mean_here
    sums[head, 0:slots, channels + 1 : channels + 2] = square_here

    def sums_copy(d):
        return pltpu.make_async_remote_copy(
            src_ref=sums.at[head],
            dst_ref=sums.at[head],
            send_sem=sums_send_sem.at[d],
            recv_sem=sums_recv_sem.at[head],
            device_id=(seq, head_peer(d)),
            device_id_type=MESH,
        )

    for d in range(1, n_head):
        sums_copy(d).start()
    for d in range(1, n_head):
        source = head_peer(d)
        pltpu.make_async_remote_copy(
            src_ref=sums.at[source],
            dst_ref=sums.at[source],
            send_sem=sums_send_sem.at[0],
            recv_sem=sums_recv_sem.at[source],
            device_id=(seq, source),
            device_id_type=MESH,
        ).wait_recv()

    means = [sums[i, 0:slots, channels : channels + 1] for i in range(n_head)]
    mean = sum(means[1:], means[0]) / n_head
    squares = jnp.zeros((slots, 1), jnp.float32)
    fresh = jnp.zeros((slots, channels), jnp.float32)
    offset = jnp.zeros((1, channels), jnp.float32)
    for i in range(n_head):
        away = means[i] - mean
        squares = squares + sums[i, 0:slots, channels + 1 : channels + 2] + share * away * away
        column = sums[i, slots : slots + 1, 0:channels]
        fresh = fresh + sums[i, 0:slots, 0:channels] + away * column
        offset = offset + sums[i, slots + 1 : slots + 2, 0:channels]
    fresh = fresh * lax.rsqrt(squares / model + EPS) + offset
    chosen[...] = jnp.transpose(
        jnp.dot(one_hot, fresh, precision=HIGH, preferred_element_type=jnp.float32)
    )

    if pair == 2:
        kv_copy(0).wait_send()
        kv_copy(1).wait_send()

    def drain(d, carry):
        q_copy(d).wait_send()
        part_copy(d).wait_send()
        stat_copy(d).wait_send()
        return carry

    loop(1, groups, drain, 0)
    for d in range(1, n_head):
        cols_copy(d).wait_send()
        sums_copy(d).wait_send()


def on_device(
    n_seq,
    n_head,
    query,
    new_kv,
    cache_kv,
    text_kv,
    active,
    counts,
    hidden,
    w_out,
    mod_shift,
    mod_scale,
    w_final,
    latent,
    cached_velocity,
    step_size,
):
    slots, width = query.shape
    tokens = cache_kv.shape[1]
    share = hidden.shape[1]
    channels = w_final.shape[1]
    pair = 2 if n_seq % 2 == 0 else 1
    groups = n_seq // pair
    vmem = pl.BlockSpec(memory_space=pltpu.VMEM)
    hbm = pl.BlockSpec(memory_space=pltpu.HBM)
    dma = pltpu.SemaphoreType.DMA
    flops = 2 * slots * (2 * width * (n_seq * tokens + text_kv.shape[1]) + width * share * n_head)
    chosen, renewed = pl.pallas_call(
        functools.partial(kernel, n_seq, n_head, pair),
        out_shape=(
            jax.ShapeDtypeStruct((channels, tokens), jnp.float32),
            jax.ShapeDtypeStruct((channels, tokens), jnp.float32),
        ),
        in_specs=[hbm] * 11,
        out_specs=(vmem, vmem),
        scratch_shapes=[
            pltpu.VMEM(query.shape, jnp.bfloat16),
            pltpu.VMEM(new_kv.shape, jnp.bfloat16),
            pltpu.VMEM(cache_kv.shape, jnp.bfloat16),
            pltpu.VMEM((1, slots), jnp.int32),
            pltpu.SMEM((1,), jnp.int32),
            pltpu.VMEM(hidden.shape, jnp.bfloat16),
            pltpu.VMEM((share // 128, 128), jnp.float32),
            pltpu.VMEM((share // 128, 128), jnp.float32),
            pltpu.VMEM((channels, share), jnp.float32),
            pltpu.VMEM((groups, slots, width), jnp.bfloat16),
            pltpu.VMEM((2, pair, tokens, width), jnp.bfloat16),
            pltpu.VMEM(text_kv.shape, jnp.bfloat16),
            pltpu.VMEM((n_head, width, share), jnp.bfloat16),
            pltpu.VMEM((groups, slots, width), jnp.bfloat16),
            pltpu.VMEM((groups, slots, width), jnp.bfloat16),
            pltpu.VMEM((groups, 8, slots), jnp.float32),
            pltpu.VMEM((groups, 8, slots), jnp.float32),
            pltpu.VMEM((n_head, slots, share), jnp.bfloat16),
            pltpu.VMEM((n_head, slots, share), jnp.bfloat16),
            pltpu.VMEM((n_head, slots + 8, 128), jnp.float32),
            dma((10 + n_head,)),
            dma((2,)),
            dma((2,)),
            dma((groups,)),
            dma((groups,)),
            dma((groups,)),
            dma((groups,)),
            dma((groups,)),
            dma((groups,)),
            dma((n_head,)),
            dma((n_head,)),
            dma((n_head,)),
            dma((n_head,)),
        ],
        compiler_params=pltpu.CompilerParams(
            collective_id=0, has_side_effects=True, vmem_limit_bytes=60 * 1024 * 1024
        ),
        cost_estimate=pl.CostEstimate(
            flops=flops, bytes_accessed=2 * w_out.size, transcendentals=0
        ),
    )(
        query,
        new_kv,
        cache_kv,
        text_kv,
        active.reshape(1, slots),
        counts,
        hidden,
        w_out,
        mod_shift.reshape(share // 128, 128),
        mod_scale.reshape(share // 128, 128),
        w_final.T,
    )
    velocity = jnp.where(renewed > 0.5, chosen, cached_velocity.T)
    latent_next = latent.T + step_size[0] * velocity
    return (velocity.T, latent_next.T)


def solution(mesh):
    in_specs = (
        P("seq", "head"),
        P(None, "seq", "head"),
        P(None, "seq", "head"),
        P(None, None, "head"),
        P("seq"),
        P("seq"),
        P("seq", "head"),
        P("head", None),
        P("head"),
        P("head"),
        P("head", None),
        P("seq", None),
        P("seq", None),
        P(),
    )
    out_specs = (P("seq", None), P("seq", None))
    return jax.shard_map(
        functools.partial(on_device, mesh.shape["seq"], mesh.shape["head"]),
        mesh=mesh,
        in_specs=in_specs,
        out_specs=out_specs,
        check_vma=False,
    )
```

```python
import functools

import jax
import jax.numpy as jnp
from jax import lax
from jax.experimental import pallas as pl
from jax.experimental.pallas import tpu as pltpu
from jax.sharding import PartitionSpec as P

HD = 128
EPS = 1e-06
MESH = pl.DeviceIdType.MESH


def loop(first, last, body, carry):
    if last - first <= 8:
        for d in range(first, last):
            carry = body(d, carry)
        return carry
    return lax.fori_loop(first, last, body, carry)


def kernel(
    n_seq,
    n_head,
    pair,
    query_hbm,
    new_kv_hbm,
    cache_kv_hbm,
    text_hbm,
    active_hbm,
    counts_hbm,
    hidden_hbm,
    w_out_hbm,
    mod_shift_hbm,
    mod_scale_hbm,
    w_final_hbm,
    latent_hbm,
    cached_velocity_hbm,
    step_size_hbm,
    result,
    new_kv,
    cache_kv,
    active,
    counts,
    hidden,
    mod_shift,
    mod_scale,
    w_final,
    latent,
    cached_velocity,
    step_size,
    q_all,
    kv,
    text,
    w_out,
    part_send,
    part_recv,
    stat_send,
    stat_recv,
    cols_send,
    cols_recv,
    sums,
    local_sem,
    kv_send_sem,
    kv_recv_sem,
    q_send_sem,
    q_recv_sem,
    part_send_sem,
    part_recv_sem,
    stat_send_sem,
    stat_recv_sem,
    cols_send_sem,
    cols_recv_sem,
    sums_send_sem,
    sums_recv_sem,
):
    seq = lax.axis_index("seq")
    head = lax.axis_index("head")
    slots, width = query_hbm.shape
    tokens = cache_kv.shape[1]
    heads = width // HD
    groups = n_seq // pair
    group = seq // pair
    place = seq % pair
    model = n_head * hidden.shape[1]
    share = hidden.shape[1]
    channels = w_final.shape[0]

    def group_peer(d):
        return lax.rem(group + d, groups)

    cores = 2 if n_head % 2 == 0 else 1
    chips = n_head // cores

    def head_peer(d):
        chip = lax.rem(head // cores + d // cores, chips)
        return chip * cores + lax.rem(head % cores + d % cores, cores)

    barrier = pltpu.get_barrier_semaphore()

    def greet(d, carry):
        pl.semaphore_signal(
            barrier, inc=1, device_id=(group_peer(d) * pair + place, head), device_id_type=MESH
        )
        return carry

    loop(1, groups, greet, 0)
    partner = group * pair + (pair - 1 - place)
    if pair == 2:
        pl.semaphore_signal(barrier, inc=1, device_id=(partner, head), device_id_type=MESH)
    for d in range(1, n_head):
        pl.semaphore_signal(barrier, inc=1, device_id=(seq, head_peer(d)), device_id_type=MESH)

    local = []

    def fetch(source, target):
        copy = pltpu.make_async_copy(source, target, local_sem.at[len(local)])
        copy.start()
        local.append(copy)
        return copy

    first_in = [
        fetch(query_hbm, q_all.at[group]),
        fetch(active_hbm, active),
        fetch(counts_hbm, counts),
        fetch(new_kv_hbm, new_kv),
        fetch(cache_kv_hbm, cache_kv),
    ]
    text_in = fetch(text_hbm, text)
    norm_in = [
        fetch(mod_shift_hbm, mod_shift),
        fetch(mod_scale_hbm, mod_scale),
        fetch(w_final_hbm, w_final),
    ]
    w_out_in = [None] * n_head
    for d in reversed(range(n_head)):
        at = pl.ds(pl.multiple_of(head_peer(d) * share, 128), share)
        w_out_in[d] = fetch(w_out_hbm.at[:, at], w_out.at[d])
    hidden_in = fetch(hidden_hbm, hidden)
    last_in = [
        fetch(latent_hbm, latent),
        fetch(cached_velocity_hbm, cached_velocity),
        fetch(step_size_hbm, step_size),
    ]
    for copy in first_in:
        copy.wait()

    positions = active[...] - seq * tokens
    slot_ids = lax.broadcasted_iota(jnp.int32, (1, slots), 1)
    positions = jnp.where(slot_ids < counts[...], positions, -1)
    matched = lax.broadcasted_iota(jnp.int32, (tokens, slots), 0) == positions
    one_hot = matched.astype(jnp.float32)
    replaced = jnp.max(one_hot, axis=1, keepdims=True) > 0.5

    def place_rows(which):
        placed = jnp.dot(
            one_hot.astype(jnp.bfloat16), new_kv[which], preferred_element_type=jnp.float32
        )
        own = cache_kv[which].astype(jnp.float32)
        kv[which, 0] = jnp.where(replaced, placed, own).astype(jnp.bfloat16)

    place_rows(0)
    place_rows(1)
    pl.semaphore_wait(barrier, groups - 1 + pair - 1 + n_head - 1)

    def q_copy(d):
        return pltpu.make_async_remote_copy(
            src_ref=q_all.at[group],
            dst_ref=q_all.at[group],
            send_sem=q_send_sem.at[d],
            recv_sem=q_recv_sem.at[group],
            device_id=(group_peer(d) * pair + place, head),
            device_id_type=MESH,
        )

    def kv_copy(which):
        return pltpu.make_async_remote_copy(
            src_ref=kv.at[which, 0],
            dst_ref=kv.at[which, 1],
            send_sem=kv_send_sem.at[which],
            recv_sem=kv_recv_sem.at[which],
            device_id=(partner, head),
            device_id_type=MESH,
        )

    def start_q(d, carry):
        q_copy(d).start()
        return carry

    if pair == 2:
        kv_copy(0).start()
    loop(1, groups, start_q, 0)
    if pair == 2:
        kv_copy(1).start()

    def weigh(rows, keys, h):
        at = slice(h * HD, (h + 1) * HD)
        scores = lax.dot_general(
            rows[:, at],
            keys[:, at],
            (((1,), (1,)), ((), ())),
            preferred_element_type=jnp.float32,
        ) * HD ** (-0.5)
        top = jnp.max(scores, axis=1, keepdims=True)
        weights = jnp.exp(scores - top)
        total = jnp.sum(weights, axis=1, keepdims=True)
        return weights.astype(jnp.bfloat16), top, total

    def blend_of(weights, values, h):
        return jnp.dot(
            weights,
            values[:, h * HD : (h + 1) * HD],
            preferred_element_type=jnp.float32,
        )

    def merge(first, second):
        result = []
        for (blend_a, top_a, total_a), (blend_b, top_b, total_b) in zip(first, second):
            top = jnp.maximum(top_a, top_b)
            share_a, share_b = jnp.exp(top_a - top), jnp.exp(top_b - top)
            result.append(
                (
                    blend_a * share_a + blend_b * share_b,
                    top,
                    total_a * share_a + total_b * share_b,
                )
            )
        return result

    for copy in norm_in:
        copy.wait()

    def as_row(ref):
        return jnp.concatenate([ref[i : i + 1, :] for i in range(ref.shape[0])], axis=1)

    lifted = 1.0 + as_row(mod_scale)

    def split(x):
        top = x.astype(jnp.bfloat16)
        return top, (x - top.astype(jnp.float32)).astype(jnp.bfloat16)

    final_top, final_rest = split(w_final[...])

    def final_dot(rows):
        count = rows.shape[0]
        top, rest = split(rows)

        def times(left, right):
            return lax.dot_general(
                left, right, (((1,), (1,)), ((), ())), preferred_element_type=jnp.float32
            )

        both = times(jnp.concatenate([top, rest], axis=0), final_top)
        return both[:count] + (both[count:] + times(top, final_rest))

    rows8 = lax.broadcasted_iota(jnp.int32, (16, share), 0)
    pairs = jnp.where(rows8 == 0, lifted, jnp.where(rows8 == 1, as_row(mod_shift), 0.0))
    sums[head, slots : slots + 8, 0:channels] = final_dot(pairs)[:8]
    text_in.wait()
    state = []
    own = q_all[group]
    for h in range(heads):
        weights, top, total = weigh(own, text[0], h)
        state.append((blend_of(weights, text[1], h), top, total))

    def part_copy(to):
        return pltpu.make_async_remote_copy(
            src_ref=part_send.at[to],
            dst_ref=part_recv.at[group],
            send_sem=part_send_sem.at[to],
            recv_sem=part_recv_sem.at[group],
            device_id=(to * pair + place, head),
            device_id_type=MESH,
        )

    def stat_copy(to):
        return pltpu.make_async_remote_copy(
            src_ref=stat_send.at[to],
            dst_ref=stat_recv.at[group],
            send_sem=stat_send_sem.at[to],
            recv_sem=stat_recv_sem.at[group],
            device_id=(to * pair + place, head),
            device_id_type=MESH,
        )

    def arrived(buffer, sems, source):
        pltpu.make_async_remote_copy(
            src_ref=buffer.at[source],
            dst_ref=buffer.at[source],
            send_sem=q_send_sem.at[0],
            recv_sem=sems.at[source],
            device_id=(source * pair + place, head),
            device_id_type=MESH,
        ).wait_recv()

    batch = min(groups, 4) if groups % 4 == 0 or groups < 4 else 1
    lanes = lax.broadcasted_iota(jnp.int32, (batch * slots, HD), 1)

    def answer(step, carry):
        first = step * batch
        for i in range(batch):

            @pl.when(first + i != group)
            def _():
                arrived(q_all, q_recv_sem, first + i)

        if pair == 2:

            @pl.when(first == 0)
            def _():
                kv_copy(0).wait_recv()

        keys = kv[0].reshape(pair * tokens, width)
        rows = q_all[pl.ds(first, batch)].reshape(batch * slots, width)
        weighed = [weigh(rows, keys, h) for h in range(heads)]
        spread = jnp.zeros((batch * slots, HD), jnp.float32)
        for h, (_, top, total) in enumerate(weighed):
            spread = jnp.where(lanes == h, top + jnp.log(total), spread)
        for i in range(batch):
            stat_send[first + i] = jnp.transpose(spread[i * slots : (i + 1) * slots])[:8]
        inverse = [1.0 / total for _, _, total in weighed]
        if pair == 2:

            @pl.when(first == 0)
            def _():
                kv_copy(1).wait_recv()

        values = kv[1].reshape(pair * tokens, width)
        for h, (weights, _, _) in enumerate(weighed):
            at = slice(h * HD, (h + 1) * HD)
            blend = (blend_of(weights, values, h) * inverse[h]).astype(jnp.bfloat16)
            for i in range(batch):
                part_send[first + i, :, at] = blend[i * slots : (i + 1) * slots]
        for i in range(batch):

            @pl.when(first + i != group)
            def _():
                stat_copy(first + i).start()
                part_copy(first + i).start()

        return carry

    loop(0, groups // batch, answer, 0)

    def taken(buffer, stats, source):
        spread = jnp.transpose(stats[source])
        return [
            (
                buffer[source, :, h * HD : (h + 1) * HD].astype(jnp.float32),
                spread[:, h : h + 1],
                jnp.ones((slots, 1), jnp.float32),
            )
            for h in range(heads)
        ]

    state = merge(state, taken(part_send, stat_send, group))

    def gather(d, carry):
        source = lax.rem(group + groups - d, groups)
        arrived(stat_recv, stat_recv_sem, source)
        arrived(part_recv, part_recv_sem, source)
        return merge(carry, taken(part_recv, stat_recv, source))

    state = loop(1, groups, gather, state)
    attended = jnp.concatenate(
        [(blend / total).astype(jnp.bfloat16) for blend, top, total in state], axis=1
    )

    def cols_copy(d):
        return pltpu.make_async_remote_copy(
            src_ref=cols_send.at[d],
            dst_ref=cols_recv.at[d],
            send_sem=cols_send_sem.at[d],
            recv_sem=cols_recv_sem.at[d],
            device_id=(seq, head_peer(d)),
            device_id_type=MESH,
        )

    for d in reversed(range(1, n_head)):
        w_out_in[d].wait()
        cols_send[d] = jnp.dot(attended, w_out[d], preferred_element_type=jnp.float32).astype(
            jnp.bfloat16
        )
        cols_copy(d).start()
    w_out_in[0].wait()
    hidden_in.wait()
    residual = hidden[...].astype(jnp.float32) + jnp.dot(
        attended, w_out[0], preferred_element_type=jnp.float32
    )
    for copy in last_in:
        copy.wait()
    for d in range(1, n_head):
        cols_copy(d).wait_recv()
        residual = residual + cols_recv[d].astype(jnp.float32)

    mean_here = jnp.sum(residual, axis=1, keepdims=True) / share
    centred = residual - mean_here
    square_here = jnp.sum(centred * centred, axis=1, keepdims=True)
    scaled = final_dot(centred * lifted)
    sums[head, 0:slots, 0:channels] = scaled
    sums[head, 0:slots, channels : channels + 1] = mean_here
    sums[head, 0:slots, channels + 1 : channels + 2] = square_here

    def sums_copy(d):
        return pltpu.make_async_remote_copy(
            src_ref=sums.at[head],
            dst_ref=sums.at[head],
            send_sem=sums_send_sem.at[d],
            recv_sem=sums_recv_sem.at[head],
            device_id=(seq, head_peer(d)),
            device_id_type=MESH,
        )

    for d in reversed(range(1, n_head)):
        sums_copy(d).start()
    for d in range(1, n_head):
        source = head_peer(d)
        pltpu.make_async_remote_copy(
            src_ref=sums.at[source],
            dst_ref=sums.at[source],
            send_sem=sums_send_sem.at[0],
            recv_sem=sums_recv_sem.at[source],
            device_id=(seq, source),
            device_id_type=MESH,
        ).wait_recv()

    means = [sums[i, 0:slots, channels : channels + 1] for i in range(n_head)]
    mean = sum(means[1:], means[0]) / n_head
    squares = jnp.zeros((slots, 1), jnp.float32)
    fresh = jnp.zeros((slots, channels), jnp.float32)
    offset = jnp.zeros((1, channels), jnp.float32)
    for i in range(n_head):
        away = means[i] - mean
        squares = squares + sums[i, 0:slots, channels + 1 : channels + 2] + share * away * away
        column = sums[i, slots : slots + 1, 0:channels]
        fresh = fresh + sums[i, 0:slots, 0:channels] + away * column
        offset = offset + sums[i, slots + 1 : slots + 2, 0:channels]
    fresh = fresh * lax.rsqrt(squares / model + EPS) + offset
    parts, rest = [], fresh
    for _ in range(3):
        parts.append(rest.astype(jnp.bfloat16))
        rest = rest - parts[-1].astype(jnp.float32)
    mask = one_hot.astype(jnp.bfloat16)
    chosen = [jnp.dot(mask, part, preferred_element_type=jnp.float32) for part in parts]
    chosen = chosen[0] + (chosen[1] + chosen[2])
    chosen = jnp.transpose(jnp.where(replaced, chosen, jnp.transpose(cached_velocity[...])))
    result[0] = chosen
    result[1] = latent[...] + step_size[...] * chosen

    if pair == 2:
        kv_copy(0).wait_send()
        kv_copy(1).wait_send()

    def drain(d, carry):
        q_copy(d).wait_send()
        part_copy(group_peer(d)).wait_send()
        stat_copy(group_peer(d)).wait_send()
        return carry

    loop(1, groups, drain, 0)
    for d in range(1, n_head):
        cols_copy(d).wait_send()
        sums_copy(d).wait_send()


def on_device(
    n_seq,
    n_head,
    query,
    new_kv,
    cache_kv,
    text_kv,
    active,
    counts,
    hidden,
    w_out,
    mod_shift,
    mod_scale,
    w_final,
    latent,
    cached_velocity,
    step_size,
):
    slots, width = query.shape
    tokens = cache_kv.shape[1]
    share = hidden.shape[1]
    channels = w_final.shape[1]
    pair = 2 if n_seq % 2 == 0 else 1
    groups = n_seq // pair
    vmem = pl.BlockSpec(memory_space=pltpu.VMEM)
    hbm = pl.BlockSpec(memory_space=pltpu.HBM)
    dma = pltpu.SemaphoreType.DMA
    flops = 2 * slots * (2 * width * (n_seq * tokens + text_kv.shape[1]) + width * share * n_head)
    result = pl.pallas_call(
        functools.partial(kernel, n_seq, n_head, pair),
        out_shape=jax.ShapeDtypeStruct((2, channels, tokens), jnp.float32),
        in_specs=[hbm] * 14,
        out_specs=vmem,
        scratch_shapes=[
            pltpu.VMEM(new_kv.shape, jnp.bfloat16),
            pltpu.VMEM(cache_kv.shape, jnp.bfloat16),
            pltpu.VMEM((1, slots), jnp.int32),
            pltpu.VMEM((1, 1), jnp.int32),
            pltpu.VMEM(hidden.shape, jnp.bfloat16),
            pltpu.VMEM((share // 128, 128), jnp.float32),
            pltpu.VMEM((share // 128, 128), jnp.float32),
            pltpu.VMEM((channels, share), jnp.float32),
            pltpu.VMEM((channels, tokens), jnp.float32),
            pltpu.VMEM((channels, tokens), jnp.float32),
            pltpu.VMEM((1, 1), jnp.float32),
            pltpu.VMEM((groups, slots, width), jnp.bfloat16),
            pltpu.VMEM((2, pair, tokens, width), jnp.bfloat16),
            pltpu.VMEM(text_kv.shape, jnp.bfloat16),
            pltpu.VMEM((n_head, width, share), jnp.bfloat16),
            pltpu.VMEM((groups, slots, width), jnp.bfloat16),
            pltpu.VMEM((groups, slots, width), jnp.bfloat16),
            pltpu.VMEM((groups, 8, slots), jnp.float32),
            pltpu.VMEM((groups, 8, slots), jnp.float32),
            pltpu.VMEM((n_head, slots, share), jnp.bfloat16),
            pltpu.VMEM((n_head, slots, share), jnp.bfloat16),
            pltpu.VMEM((n_head, slots + 8, 128), jnp.float32),
            dma((13 + n_head,)),
            dma((2,)),
            dma((2,)),
            dma((groups,)),
            dma((groups,)),
            dma((groups,)),
            dma((groups,)),
            dma((groups,)),
            dma((groups,)),
            dma((n_head,)),
            dma((n_head,)),
            dma((n_head,)),
            dma((n_head,)),
        ],
        compiler_params=pltpu.CompilerParams(
            collective_id=0, has_side_effects=True, vmem_limit_bytes=60 * 1024 * 1024
        ),
        cost_estimate=pl.CostEstimate(
            flops=flops, bytes_accessed=2 * w_out.size, transcendentals=0
        ),
    )(
        query,
        new_kv,
        cache_kv,
        text_kv,
        active.reshape(1, slots),
        counts.reshape(1, 1),
        hidden,
        w_out,
        mod_shift.reshape(share // 128, 128),
        mod_scale.reshape(share // 128, 128),
        w_final.T,
        latent.T,
        cached_velocity.T,
        step_size.reshape(1, 1),
    )
    return (result[0].T, result[1].T)


def solution(mesh):
    in_specs = (
        P("seq", "head"),
        P(None, "seq", "head"),
        P(None, "seq", "head"),
        P(None, None, "head"),
        P("seq"),
        P("seq"),
        P("seq", "head"),
        P("head", None),
        P("head"),
        P("head"),
        P("head", None),
        P("seq", None),
        P("seq", None),
        P(),
    )
    out_specs = (P("seq", None), P("seq", None))
    return jax.shard_map(
        functools.partial(on_device, mesh.shape["seq"], mesh.shape["head"]),
        mesh=mesh,
        in_specs=in_specs,
        out_specs=out_specs,
        check_vma=False,
    )
```

```python
import functools

import jax
import jax.numpy as jnp
from jax import lax
from jax.experimental import pallas as pl
from jax.experimental.pallas import tpu as pltpu
from jax.sharding import PartitionSpec as P

HD = 128
EPS = 1e-06
MESH = pl.DeviceIdType.MESH


def loop(first, last, body, carry):
    if last - first <= 8:
        for d in range(first, last):
            carry = body(d, carry)
        return carry
    return lax.fori_loop(first, last, body, carry)


def kernel(
    n_seq,
    n_head,
    pair,
    query_hbm,
    new_kv_hbm,
    cache_kv_hbm,
    text_hbm,
    active_hbm,
    counts_hbm,
    hidden_hbm,
    w_out_hbm,
    mod_shift_hbm,
    mod_scale_hbm,
    w_final_hbm,
    latent_hbm,
    cached_velocity_hbm,
    step_size_hbm,
    result,
    new_kv,
    cache_kv,
    active,
    counts,
    hidden,
    mod_shift,
    mod_scale,
    w_final,
    latent,
    cached_velocity,
    step_size,
    q_all,
    kv,
    text,
    w_out,
    part_send,
    part_recv,
    stat_send,
    stat_recv,
    cols_send,
    cols_recv,
    sums,
    local_sem,
    kv_send_sem,
    kv_recv_sem,
    q_send_sem,
    q_recv_sem,
    part_send_sem,
    part_recv_sem,
    stat_send_sem,
    stat_recv_sem,
    cols_send_sem,
    cols_recv_sem,
    sums_send_sem,
    sums_recv_sem,
):
    seq = lax.axis_index("seq")
    head = lax.axis_index("head")
    slots, width = query_hbm.shape
    tokens = cache_kv.shape[1]
    heads = width // HD
    groups = n_seq // pair
    group = seq // pair
    place = seq % pair
    model = n_head * hidden.shape[1]
    share = hidden.shape[1]
    channels = w_final.shape[0]

    def group_peer(d):
        return lax.rem(group + d, groups)

    cores = 2 if n_head % 2 == 0 else 1
    chips = n_head // cores

    def head_peer(d):
        chip = lax.rem(head // cores + d // cores, chips)
        return chip * cores + lax.rem(head % cores + d % cores, cores)

    barrier = pltpu.get_barrier_semaphore()

    def greet(d, carry):
        pl.semaphore_signal(
            barrier, inc=1, device_id=(group_peer(d) * pair + place, head), device_id_type=MESH
        )
        return carry

    loop(1, groups, greet, 0)
    partner = group * pair + (pair - 1 - place)
    if pair == 2:
        pl.semaphore_signal(barrier, inc=1, device_id=(partner, head), device_id_type=MESH)
    for d in range(1, n_head):
        pl.semaphore_signal(barrier, inc=1, device_id=(seq, head_peer(d)), device_id_type=MESH)

    def cut(h):
        return slice(h * HD, (h + 1) * HD)

    local = []

    def fetch(source, target):
        copy = pltpu.make_async_copy(source, target, local_sem.at[len(local)])
        copy.start()
        local.append(copy)
        return copy

    first_in = [
        *[fetch(query_hbm.at[:, cut(h)], q_all.at[h, group]) for h in range(heads)],
        fetch(active_hbm, active),
        fetch(counts_hbm, counts),
        fetch(new_kv_hbm, new_kv),
        fetch(cache_kv_hbm, cache_kv),
    ]
    text_in = fetch(text_hbm, text)
    norm_in = [
        fetch(mod_shift_hbm, mod_shift),
        fetch(mod_scale_hbm, mod_scale),
        fetch(w_final_hbm, w_final),
    ]
    w_out_in = [None] * n_head
    for d in reversed(range(n_head)):
        at = pl.ds(pl.multiple_of(head_peer(d) * share, 128), share)
        w_out_in[d] = fetch(w_out_hbm.at[:, at], w_out.at[d])
    hidden_in = fetch(hidden_hbm, hidden)
    last_in = [
        fetch(latent_hbm, latent),
        fetch(cached_velocity_hbm, cached_velocity),
        fetch(step_size_hbm, step_size),
    ]
    for copy in first_in:
        copy.wait()

    positions = active[...] - seq * tokens
    slot_ids = lax.broadcasted_iota(jnp.int32, (1, slots), 1)
    positions = jnp.where(slot_ids < counts[...], positions, -1)
    matched = lax.broadcasted_iota(jnp.int32, (tokens, slots), 0) == positions
    one_hot = matched.astype(jnp.float32)
    replaced = jnp.max(one_hot, axis=1, keepdims=True) > 0.5

    def place_rows(which):
        placed = jnp.dot(
            one_hot.astype(jnp.bfloat16), new_kv[which], preferred_element_type=jnp.float32
        )
        own = cache_kv[which].astype(jnp.float32)
        merged = jnp.where(replaced, placed, own).astype(jnp.bfloat16)
        for h in range(heads):
            kv[h, 0, which] = merged[:, cut(h)]

    place_rows(0)
    place_rows(1)
    pl.semaphore_wait(barrier, groups - 1 + pair - 1 + n_head - 1)

    def q_copy(h, d):
        return pltpu.make_async_remote_copy(
            src_ref=q_all.at[h, group],
            dst_ref=q_all.at[h, group],
            send_sem=q_send_sem.at[h, d],
            recv_sem=q_recv_sem.at[h, group],
            device_id=(group_peer(d) * pair + place, head),
            device_id_type=MESH,
        )

    def kv_copy(h):
        return pltpu.make_async_remote_copy(
            src_ref=kv.at[h, 0],
            dst_ref=kv.at[h, 1],
            send_sem=kv_send_sem.at[h],
            recv_sem=kv_recv_sem.at[h],
            device_id=(partner, head),
            device_id_type=MESH,
        )

    for h in range(heads):

        def start_q(d, carry):
            q_copy(h, d).start()
            return carry

        if pair == 2:
            kv_copy(h).start()
        loop(1, groups, start_q, 0)

    def weigh(rows, keys):
        scores = lax.dot_general(
            rows, keys, (((1,), (1,)), ((), ())), preferred_element_type=jnp.float32
        ) * HD ** (-0.5)
        top = jnp.max(scores, axis=1, keepdims=True)
        weights = jnp.exp(scores - top)
        total = jnp.sum(weights, axis=1, keepdims=True)
        return weights.astype(jnp.bfloat16), top, total

    def blend_of(weights, values):
        return jnp.dot(weights, values, preferred_element_type=jnp.float32)

    def merge(first, second):
        (blend_a, top_a, total_a), (blend_b, top_b, total_b) = first, second
        top = jnp.maximum(top_a, top_b)
        share_a, share_b = jnp.exp(top_a - top), jnp.exp(top_b - top)
        return (
            blend_a * share_a + blend_b * share_b,
            top,
            total_a * share_a + total_b * share_b,
        )

    for copy in norm_in:
        copy.wait()

    def as_row(ref):
        return jnp.concatenate([ref[i : i + 1, :] for i in range(ref.shape[0])], axis=1)

    lifted = 1.0 + as_row(mod_scale)

    def split(x):
        top = x.astype(jnp.bfloat16)
        return top, (x - top.astype(jnp.float32)).astype(jnp.bfloat16)

    final_top, final_rest = split(w_final[...])

    def final_dot(rows):
        count = rows.shape[0]
        top, rest = split(rows)

        def times(left, right):
            return lax.dot_general(
                left, right, (((1,), (1,)), ((), ())), preferred_element_type=jnp.float32
            )

        both = times(jnp.concatenate([top, rest], axis=0), final_top)
        return both[:count] + (both[count:] + times(top, final_rest))

    rows8 = lax.broadcasted_iota(jnp.int32, (16, share), 0)
    pairs = jnp.where(rows8 == 0, lifted, jnp.where(rows8 == 1, as_row(mod_shift), 0.0))
    sums[head, slots : slots + 8, 0:channels] = final_dot(pairs)[:8]
    text_in.wait()
    state = []
    for h in range(heads):
        weights, top, total = weigh(q_all[h, group], text[0, :, cut(h)])
        state.append((blend_of(weights, text[1, :, cut(h)]), top, total))

    def part_copy(h, to):
        return pltpu.make_async_remote_copy(
            src_ref=part_send.at[h, to],
            dst_ref=part_recv.at[h, group],
            send_sem=part_send_sem.at[h, to],
            recv_sem=part_recv_sem.at[h, group],
            device_id=(to * pair + place, head),
            device_id_type=MESH,
        )

    def stat_copy(h, to):
        return pltpu.make_async_remote_copy(
            src_ref=stat_send.at[h, to],
            dst_ref=stat_recv.at[h, group],
            send_sem=stat_send_sem.at[h, to],
            recv_sem=stat_recv_sem.at[h, group],
            device_id=(to * pair + place, head),
            device_id_type=MESH,
        )

    def arrived(buffer, sems, h, source):
        pltpu.make_async_remote_copy(
            src_ref=buffer.at[h, source],
            dst_ref=buffer.at[h, source],
            send_sem=q_send_sem.at[h, 0],
            recv_sem=sems.at[h, source],
            device_id=(source * pair + place, head),
            device_id_type=MESH,
        ).wait_recv()

    batch = min(groups, 4) if groups % 4 == 0 or groups < 4 else 1

    for h in range(heads):
        if pair == 2:
            kv_copy(h).wait_recv()

        def answer(step, carry):
            first = step * batch
            for i in range(batch):

                @pl.when(first + i != group)
                def _():
                    arrived(q_all, q_recv_sem, h, first + i)

            rows = q_all[h, pl.ds(first, batch)].reshape(batch * slots, HD)
            weights, top, total = weigh(rows, kv[h, :, 0].reshape(pair * tokens, HD))
            blend = blend_of(weights, kv[h, :, 1].reshape(pair * tokens, HD))
            blend = (blend * (1.0 / total)).astype(jnp.bfloat16)
            spread = jnp.broadcast_to(top + jnp.log(total), (batch * slots, HD))
            for i in range(batch):
                at = slice(i * slots, (i + 1) * slots)
                part_send[h, first + i] = blend[at]
                stat_send[h, first + i] = jnp.transpose(spread[at])[:8]
            for i in range(batch):

                @pl.when(first + i != group)
                def _():
                    stat_copy(h, first + i).start()
                    part_copy(h, first + i).start()

            return carry

        loop(0, groups // batch, answer, 0)

    def taken(buffer, stats, h, source):
        spread = jnp.transpose(stats[h, source])
        return (
            buffer[h, source].astype(jnp.float32),
            spread[:, :1],
            jnp.ones((slots, 1), jnp.float32),
        )

    attended = []
    for h in range(heads):

        def gather(d, carry):
            source = lax.rem(group + groups - d, groups)
            arrived(stat_recv, stat_recv_sem, h, source)
            arrived(part_recv, part_recv_sem, h, source)
            return merge(carry, taken(part_recv, stat_recv, h, source))

        merged = merge(state[h], taken(part_send, stat_send, h, group))
        blend, _, total = loop(1, groups, gather, merged)
        attended.append((blend / total).astype(jnp.bfloat16))
    attended = jnp.concatenate(attended, axis=1)

    def cols_copy(d):
        return pltpu.make_async_remote_copy(
            src_ref=cols_send.at[d],
            dst_ref=cols_recv.at[d],
            send_sem=cols_send_sem.at[d],
            recv_sem=cols_recv_sem.at[d],
            device_id=(seq, head_peer(d)),
            device_id_type=MESH,
        )

    for d in reversed(range(1, n_head)):
        w_out_in[d].wait()
        cols_send[d] = jnp.dot(attended, w_out[d], preferred_element_type=jnp.float32).astype(
            jnp.bfloat16
        )
        cols_copy(d).start()
    w_out_in[0].wait()
    hidden_in.wait()
    residual = hidden[...].astype(jnp.float32) + jnp.dot(
        attended, w_out[0], preferred_element_type=jnp.float32
    )
    for copy in last_in:
        copy.wait()
    for d in range(1, n_head):
        cols_copy(d).wait_recv()
        residual = residual + cols_recv[d].astype(jnp.float32)

    mean_here = jnp.sum(residual, axis=1, keepdims=True) / share
    centred = residual - mean_here
    square_here = jnp.sum(centred * centred, axis=1, keepdims=True)
    scaled = final_dot(centred * lifted)
    sums[head, 0:slots, 0:channels] = scaled
    sums[head, 0:slots, channels : channels + 1] = mean_here
    sums[head, 0:slots, channels + 1 : channels + 2] = square_here

    def sums_copy(d):
        return pltpu.make_async_remote_copy(
            src_ref=sums.at[head],
            dst_ref=sums.at[head],
            send_sem=sums_send_sem.at[d],
            recv_sem=sums_recv_sem.at[head],
            device_id=(seq, head_peer(d)),
            device_id_type=MESH,
        )

    for d in reversed(range(1, n_head)):
        sums_copy(d).start()
    for d in range(1, n_head):
        source = head_peer(d)
        pltpu.make_async_remote_copy(
            src_ref=sums.at[source],
            dst_ref=sums.at[source],
            send_sem=sums_send_sem.at[0],
            recv_sem=sums_recv_sem.at[source],
            device_id=(seq, source),
            device_id_type=MESH,
        ).wait_recv()

    means = [sums[i, 0:slots, channels : channels + 1] for i in range(n_head)]
    mean = sum(means[1:], means[0]) / n_head
    squares = jnp.zeros((slots, 1), jnp.float32)
    fresh = jnp.zeros((slots, channels), jnp.float32)
    offset = jnp.zeros((1, channels), jnp.float32)
    for i in range(n_head):
        away = means[i] - mean
        squares = squares + sums[i, 0:slots, channels + 1 : channels + 2] + share * away * away
        column = sums[i, slots : slots + 1, 0:channels]
        fresh = fresh + sums[i, 0:slots, 0:channels] + away * column
        offset = offset + sums[i, slots + 1 : slots + 2, 0:channels]
    fresh = fresh * lax.rsqrt(squares / model + EPS) + offset
    parts, rest = [], fresh
    for _ in range(3):
        parts.append(rest.astype(jnp.bfloat16))
        rest = rest - parts[-1].astype(jnp.float32)
    mask = one_hot.astype(jnp.bfloat16)
    chosen = [jnp.dot(mask, part, preferred_element_type=jnp.float32) for part in parts]
    chosen = chosen[0] + (chosen[1] + chosen[2])
    chosen = jnp.transpose(jnp.where(replaced, chosen, jnp.transpose(cached_velocity[...])))
    result[0] = chosen
    result[1] = latent[...] + step_size[...] * chosen

    for h in range(heads):

        def drain(d, carry):
            q_copy(h, d).wait_send()
            part_copy(h, group_peer(d)).wait_send()
            stat_copy(h, group_peer(d)).wait_send()
            return carry

        if pair == 2:
            kv_copy(h).wait_send()
        loop(1, groups, drain, 0)
    for d in range(1, n_head):
        cols_copy(d).wait_send()
        sums_copy(d).wait_send()


def on_device(
    n_seq,
    n_head,
    query,
    new_kv,
    cache_kv,
    text_kv,
    active,
    counts,
    hidden,
    w_out,
    mod_shift,
    mod_scale,
    w_final,
    latent,
    cached_velocity,
    step_size,
):
    slots, width = query.shape
    tokens = cache_kv.shape[1]
    share = hidden.shape[1]
    channels = w_final.shape[1]
    pair = 2 if n_seq % 2 == 0 else 1
    groups = n_seq // pair
    heads = width // HD
    vmem = pl.BlockSpec(memory_space=pltpu.VMEM)
    hbm = pl.BlockSpec(memory_space=pltpu.HBM)
    dma = pltpu.SemaphoreType.DMA
    flops = 2 * slots * (2 * width * (n_seq * tokens + text_kv.shape[1]) + width * share * n_head)
    result = pl.pallas_call(
        functools.partial(kernel, n_seq, n_head, pair),
        out_shape=jax.ShapeDtypeStruct((2, channels, tokens), jnp.float32),
        in_specs=[hbm] * 14,
        out_specs=vmem,
        scratch_shapes=[
            pltpu.VMEM(new_kv.shape, jnp.bfloat16),
            pltpu.VMEM(cache_kv.shape, jnp.bfloat16),
            pltpu.VMEM((1, slots), jnp.int32),
            pltpu.VMEM((1, 1), jnp.int32),
            pltpu.VMEM(hidden.shape, jnp.bfloat16),
            pltpu.VMEM((share // 128, 128), jnp.float32),
            pltpu.VMEM((share // 128, 128), jnp.float32),
            pltpu.VMEM((channels, share), jnp.float32),
            pltpu.VMEM((channels, tokens), jnp.float32),
            pltpu.VMEM((channels, tokens), jnp.float32),
            pltpu.VMEM((1, 1), jnp.float32),
            pltpu.VMEM((heads, groups, slots, HD), jnp.bfloat16),
            pltpu.VMEM((heads, pair, 2, tokens, HD), jnp.bfloat16),
            pltpu.VMEM(text_kv.shape, jnp.bfloat16),
            pltpu.VMEM((n_head, width, share), jnp.bfloat16),
            pltpu.VMEM((heads, groups, slots, HD), jnp.bfloat16),
            pltpu.VMEM((heads, groups, slots, HD), jnp.bfloat16),
            pltpu.VMEM((heads, groups, 8, slots), jnp.float32),
            pltpu.VMEM((heads, groups, 8, slots), jnp.float32),
            pltpu.VMEM((n_head, slots, share), jnp.bfloat16),
            pltpu.VMEM((n_head, slots, share), jnp.bfloat16),
            pltpu.VMEM((n_head, slots + 8, 128), jnp.float32),
            dma((12 + heads + n_head,)),
            dma((heads,)),
            dma((heads,)),
            dma((heads, groups)),
            dma((heads, groups)),
            dma((heads, groups)),
            dma((heads, groups)),
            dma((heads, groups)),
            dma((heads, groups)),
            dma((n_head,)),
            dma((n_head,)),
            dma((n_head,)),
            dma((n_head,)),
        ],
        compiler_params=pltpu.CompilerParams(
            collective_id=0, has_side_effects=True, vmem_limit_bytes=60 * 1024 * 1024
        ),
        cost_estimate=pl.CostEstimate(
            flops=flops, bytes_accessed=2 * w_out.size, transcendentals=0
        ),
    )(
        query,
        new_kv,
        cache_kv,
        text_kv,
        active.reshape(1, slots),
        counts.reshape(1, 1),
        hidden,
        w_out,
        mod_shift.reshape(share // 128, 128),
        mod_scale.reshape(share // 128, 128),
        w_final.T,
        latent.T,
        cached_velocity.T,
        step_size.reshape(1, 1),
    )
    return (result[0].T, result[1].T)


def solution(mesh):
    in_specs = (
        P("seq", "head"),
        P(None, "seq", "head"),
        P(None, "seq", "head"),
        P(None, None, "head"),
        P("seq"),
        P("seq"),
        P("seq", "head"),
        P("head", None),
        P("head"),
        P("head"),
        P("head", None),
        P("seq", None),
        P("seq", None),
        P(),
    )
    out_specs = (P("seq", None), P("seq", None))
    return jax.shard_map(
        functools.partial(on_device, mesh.shape["seq"], mesh.shape["head"]),
        mesh=mesh,
        in_specs=in_specs,
        out_specs=out_specs,
        check_vma=False,
    )
```

```python
import functools

import jax
import jax.numpy as jnp
from jax import lax
from jax.experimental import pallas as pl
from jax.experimental.pallas import tpu as pltpu
from jax.sharding import PartitionSpec as P

HD = 128
EPS = 1e-06
MESH = pl.DeviceIdType.MESH


def loop(first, last, body, carry):
    if last - first <= 8:
        for d in range(first, last):
            carry = body(d, carry)
        return carry
    return lax.fori_loop(first, last, body, carry)


def kernel(
    n_seq,
    n_head,
    pair,
    query_hbm,
    new_kv_hbm,
    cache_kv_hbm,
    text_hbm,
    active_hbm,
    counts_hbm,
    hidden_hbm,
    w_out_hbm,
    mod_shift_hbm,
    mod_scale_hbm,
    w_final_hbm,
    latent_hbm,
    cached_velocity_hbm,
    step_size_hbm,
    result,
    new_kv,
    cache_kv,
    active,
    counts,
    hidden,
    mod_shift,
    mod_scale,
    w_final,
    latent,
    cached_velocity,
    step_size,
    q_all,
    kv,
    text,
    w_out,
    part_send,
    part_recv,
    stat_send,
    stat_recv,
    cols_send,
    cols_recv,
    sums,
    local_sem,
    kv_send_sem,
    kv_recv_sem,
    q_send_sem,
    q_recv_sem,
    part_send_sem,
    part_recv_sem,
    stat_send_sem,
    stat_recv_sem,
    cols_send_sem,
    cols_recv_sem,
    sums_send_sem,
    sums_recv_sem,
):
    seq = lax.axis_index("seq")
    head = lax.axis_index("head")
    slots, width = query_hbm.shape
    tokens = cache_kv.shape[1]
    heads = width // HD
    groups = n_seq // pair
    group = seq // pair
    place = seq % pair
    model = n_head * hidden.shape[1]
    share = hidden.shape[1]
    channels = w_final.shape[0]

    def group_peer(d):
        return lax.rem(group + d, groups)

    cores = 2 if n_head % 2 == 0 else 1
    chips = n_head // cores

    def head_peer(d):
        chip = lax.rem(head // cores + d // cores, chips)
        return chip * cores + lax.rem(head % cores + d % cores, cores)

    barrier = pltpu.get_barrier_semaphore()

    def greet(d, carry):
        pl.semaphore_signal(
            barrier, inc=1, device_id=(group_peer(d) * pair + place, head), device_id_type=MESH
        )
        return carry

    loop(1, groups, greet, 0)
    partner = group * pair + (pair - 1 - place)
    if pair == 2:
        pl.semaphore_signal(barrier, inc=1, device_id=(partner, head), device_id_type=MESH)
    for d in range(1, n_head):
        pl.semaphore_signal(barrier, inc=1, device_id=(seq, head_peer(d)), device_id_type=MESH)

    def cut(h):
        return slice(h * HD, (h + 1) * HD)

    local = []

    def fetch(source, target):
        copy = pltpu.make_async_copy(source, target, local_sem.at[len(local)])
        copy.start()
        local.append(copy)
        return copy

    first_in = [
        *[fetch(query_hbm.at[:, cut(h)], q_all.at[h, group]) for h in range(heads)],
        fetch(active_hbm, active),
        fetch(counts_hbm, counts),
        fetch(new_kv_hbm, new_kv),
        fetch(cache_kv_hbm, cache_kv),
    ]
    text_in = fetch(text_hbm, text)
    norm_in = [
        fetch(mod_shift_hbm, mod_shift),
        fetch(mod_scale_hbm, mod_scale),
        fetch(w_final_hbm, w_final),
    ]
    w_out_in = [None] * n_head
    for d in reversed(range(n_head)):
        at = pl.ds(pl.multiple_of(head_peer(d) * share, 128), share)
        w_out_in[d] = fetch(w_out_hbm.at[:, at], w_out.at[d])
    hidden_in = fetch(hidden_hbm, hidden)
    last_in = [
        fetch(latent_hbm, latent),
        fetch(cached_velocity_hbm, cached_velocity),
        fetch(step_size_hbm, step_size),
    ]
    for copy in first_in:
        copy.wait()

    positions = active[...] - seq * tokens
    slot_ids = lax.broadcasted_iota(jnp.int32, (1, slots), 1)
    positions = jnp.where(slot_ids < counts[...], positions, -1)
    matched = lax.broadcasted_iota(jnp.int32, (tokens, slots), 0) == positions
    one_hot = matched.astype(jnp.float32)
    replaced = jnp.max(one_hot, axis=1, keepdims=True) > 0.5

    def place_rows(which):
        placed = jnp.dot(
            one_hot.astype(jnp.bfloat16), new_kv[which], preferred_element_type=jnp.float32
        )
        own = cache_kv[which].astype(jnp.float32)
        merged = jnp.where(replaced, placed, own).astype(jnp.bfloat16)
        for h in range(heads):
            kv[h, 0, which] = merged[:, cut(h)]

    place_rows(0)
    place_rows(1)
    pl.semaphore_wait(barrier, groups - 1 + pair - 1 + n_head - 1)

    def q_copy(h, d):
        return pltpu.make_async_remote_copy(
            src_ref=q_all.at[h, group],
            dst_ref=q_all.at[h, group],
            send_sem=q_send_sem.at[h, d],
            recv_sem=q_recv_sem.at[h, group],
            device_id=(group_peer(d) * pair + place, head),
            device_id_type=MESH,
        )

    def kv_copy(h):
        return pltpu.make_async_remote_copy(
            src_ref=kv.at[h, 0],
            dst_ref=kv.at[h, 1],
            send_sem=kv_send_sem.at[h],
            recv_sem=kv_recv_sem.at[h],
            device_id=(partner, head),
            device_id_type=MESH,
        )

    for h in range(heads):

        def start_q(d, carry):
            q_copy(h, d).start()
            return carry

        if pair == 2:
            kv_copy(h).start()
        loop(1, groups, start_q, 0)

    def weigh(rows, keys):
        scores = lax.dot_general(
            rows, keys, (((1,), (1,)), ((), ())), preferred_element_type=jnp.float32
        ) * HD ** (-0.5)
        top = jnp.max(scores, axis=1, keepdims=True)
        weights = jnp.exp(scores - top)
        total = jnp.sum(weights, axis=1, keepdims=True)
        return weights.astype(jnp.bfloat16), top, total

    def blend_of(weights, values):
        return jnp.dot(weights, values, preferred_element_type=jnp.float32)

    def merge(first, second):
        (blend_a, top_a, total_a), (blend_b, top_b, total_b) = first, second
        top = jnp.maximum(top_a, top_b)
        share_a, share_b = jnp.exp(top_a - top), jnp.exp(top_b - top)
        return (
            blend_a * share_a + blend_b * share_b,
            top,
            total_a * share_a + total_b * share_b,
        )

    def part_copy(h, to):
        return pltpu.make_async_remote_copy(
            src_ref=part_send.at[h, to],
            dst_ref=part_recv.at[h, group],
            send_sem=part_send_sem.at[h, to],
            recv_sem=part_recv_sem.at[h, group],
            device_id=(to * pair + place, head),
            device_id_type=MESH,
        )

    def stat_copy(h, to):
        return pltpu.make_async_remote_copy(
            src_ref=stat_send.at[h, to],
            dst_ref=stat_recv.at[h, group],
            send_sem=stat_send_sem.at[h, to],
            recv_sem=stat_recv_sem.at[h, group],
            device_id=(to * pair + place, head),
            device_id_type=MESH,
        )

    def arrived(buffer, sems, h, source):
        pltpu.make_async_remote_copy(
            src_ref=buffer.at[h, source],
            dst_ref=buffer.at[h, source],
            send_sem=q_send_sem.at[h, 0],
            recv_sem=sems.at[h, source],
            device_id=(source * pair + place, head),
            device_id_type=MESH,
        ).wait_recv()

    batch = min(groups, 4) if groups % 4 == 0 or groups < 4 else 1

    for h in range(heads):
        if pair == 2:
            kv_copy(h).wait_recv()

        def answer(step, carry):
            first = step * batch
            for i in range(batch):

                @pl.when(first + i != group)
                def _():
                    arrived(q_all, q_recv_sem, h, first + i)

            rows = q_all[h, pl.ds(first, batch)].reshape(batch * slots, HD)
            weights, top, total = weigh(rows, kv[h, :, 0].reshape(pair * tokens, HD))
            blend = blend_of(weights, kv[h, :, 1].reshape(pair * tokens, HD))
            blend = (blend * (1.0 / total)).astype(jnp.bfloat16)
            spread = jnp.broadcast_to(top + jnp.log(total), (batch * slots, HD))
            for i in range(batch):
                at = slice(i * slots, (i + 1) * slots)
                part_send[h, first + i] = blend[at]
                stat_send[h, first + i] = jnp.transpose(spread[at])[:8]
            for i in range(batch):

                @pl.when(first + i != group)
                def _():
                    stat_copy(h, first + i).start()
                    part_copy(h, first + i).start()

            return carry

        loop(0, groups // batch, answer, 0)

    for copy in norm_in:
        copy.wait()

    def as_row(ref):
        return jnp.concatenate([ref[i : i + 1, :] for i in range(ref.shape[0])], axis=1)

    lifted = 1.0 + as_row(mod_scale)

    def split(x):
        top = x.astype(jnp.bfloat16)
        return top, (x - top.astype(jnp.float32)).astype(jnp.bfloat16)

    final_top, final_rest = split(w_final[...])

    def final_dot(rows):
        count = rows.shape[0]
        top, rest = split(rows)

        def times(left, right):
            return lax.dot_general(
                left, right, (((1,), (1,)), ((), ())), preferred_element_type=jnp.float32
            )

        both = times(jnp.concatenate([top, rest], axis=0), final_top)
        return both[:count] + (both[count:] + times(top, final_rest))

    rows8 = lax.broadcasted_iota(jnp.int32, (16, share), 0)
    pairs = jnp.where(rows8 == 0, lifted, jnp.where(rows8 == 1, as_row(mod_shift), 0.0))
    sums[head, slots : slots + 8, 0:channels] = final_dot(pairs)[:8]
    text_in.wait()
    state = []
    for h in range(heads):
        weights, top, total = weigh(q_all[h, group], text[0, :, cut(h)])
        state.append((blend_of(weights, text[1, :, cut(h)]), top, total))

    def taken(buffer, stats, h, source):
        spread = jnp.transpose(stats[h, source])
        return (
            buffer[h, source].astype(jnp.float32),
            spread[:, :1],
            jnp.ones((slots, 1), jnp.float32),
        )

    attended = []
    for h in range(heads):

        def gather(d, carry):
            source = lax.rem(group + groups - d, groups)
            arrived(stat_recv, stat_recv_sem, h, source)
            arrived(part_recv, part_recv_sem, h, source)
            return merge(carry, taken(part_recv, stat_recv, h, source))

        merged = merge(state[h], taken(part_send, stat_send, h, group))
        blend, _, total = loop(1, groups, gather, merged)
        attended.append((blend / total).astype(jnp.bfloat16))
    attended = jnp.concatenate(attended, axis=1)

    def cols_copy(d):
        return pltpu.make_async_remote_copy(
            src_ref=cols_send.at[d],
            dst_ref=cols_recv.at[d],
            send_sem=cols_send_sem.at[d],
            recv_sem=cols_recv_sem.at[d],
            device_id=(seq, head_peer(d)),
            device_id_type=MESH,
        )

    for d in reversed(range(1, n_head)):
        w_out_in[d].wait()
        cols_send[d] = jnp.dot(attended, w_out[d], preferred_element_type=jnp.float32).astype(
            jnp.bfloat16
        )
        cols_copy(d).start()
    w_out_in[0].wait()
    hidden_in.wait()
    residual = hidden[...].astype(jnp.float32) + jnp.dot(
        attended, w_out[0], preferred_element_type=jnp.float32
    )
    for copy in last_in:
        copy.wait()
    for d in range(1, n_head):
        cols_copy(d).wait_recv()
        residual = residual + cols_recv[d].astype(jnp.float32)

    mean_here = jnp.sum(residual, axis=1, keepdims=True) / share
    centred = residual - mean_here
    square_here = jnp.sum(centred * centred, axis=1, keepdims=True)
    scaled = final_dot(centred * lifted)
    sums[head, 0:slots, 0:channels] = scaled
    sums[head, 0:slots, channels : channels + 1] = mean_here
    sums[head, 0:slots, channels + 1 : channels + 2] = square_here

    def sums_copy(d):
        return pltpu.make_async_remote_copy(
            src_ref=sums.at[head],
            dst_ref=sums.at[head],
            send_sem=sums_send_sem.at[d],
            recv_sem=sums_recv_sem.at[head],
            device_id=(seq, head_peer(d)),
            device_id_type=MESH,
        )

    for d in reversed(range(1, n_head)):
        sums_copy(d).start()
    for d in range(1, n_head):
        source = head_peer(d)
        pltpu.make_async_remote_copy(
            src_ref=sums.at[source],
            dst_ref=sums.at[source],
            send_sem=sums_send_sem.at[0],
            recv_sem=sums_recv_sem.at[source],
            device_id=(seq, source),
            device_id_type=MESH,
        ).wait_recv()

    means = [sums[i, 0:slots, channels : channels + 1] for i in range(n_head)]
    mean = sum(means[1:], means[0]) / n_head
    squares = jnp.zeros((slots, 1), jnp.float32)
    fresh = jnp.zeros((slots, channels), jnp.float32)
    offset = jnp.zeros((1, channels), jnp.float32)
    for i in range(n_head):
        away = means[i] - mean
        squares = squares + sums[i, 0:slots, channels + 1 : channels + 2] + share * away * away
        column = sums[i, slots : slots + 1, 0:channels]
        fresh = fresh + sums[i, 0:slots, 0:channels] + away * column
        offset = offset + sums[i, slots + 1 : slots + 2, 0:channels]
    fresh = fresh * lax.rsqrt(squares / model + EPS) + offset
    parts, rest = [], fresh
    for _ in range(3):
        parts.append(rest.astype(jnp.bfloat16))
        rest = rest - parts[-1].astype(jnp.float32)
    mask = one_hot.astype(jnp.bfloat16)
    chosen = [jnp.dot(mask, part, preferred_element_type=jnp.float32) for part in parts]
    chosen = chosen[0] + (chosen[1] + chosen[2])
    chosen = jnp.transpose(jnp.where(replaced, chosen, jnp.transpose(cached_velocity[...])))
    result[0] = chosen
    result[1] = latent[...] + step_size[...] * chosen

    for h in range(heads):

        def drain(d, carry):
            q_copy(h, d).wait_send()
            part_copy(h, group_peer(d)).wait_send()
            stat_copy(h, group_peer(d)).wait_send()
            return carry

        if pair == 2:
            kv_copy(h).wait_send()
        loop(1, groups, drain, 0)
    for d in range(1, n_head):
        cols_copy(d).wait_send()
        sums_copy(d).wait_send()


def on_device(
    n_seq,
    n_head,
    query,
    new_kv,
    cache_kv,
    text_kv,
    active,
    counts,
    hidden,
    w_out,
    mod_shift,
    mod_scale,
    w_final,
    latent,
    cached_velocity,
    step_size,
):
    slots, width = query.shape
    tokens = cache_kv.shape[1]
    share = hidden.shape[1]
    channels = w_final.shape[1]
    pair = 2 if n_seq % 2 == 0 else 1
    groups = n_seq // pair
    heads = width // HD
    vmem = pl.BlockSpec(memory_space=pltpu.VMEM)
    hbm = pl.BlockSpec(memory_space=pltpu.HBM)
    dma = pltpu.SemaphoreType.DMA
    flops = 2 * slots * (2 * width * (n_seq * tokens + text_kv.shape[1]) + width * share * n_head)
    result = pl.pallas_call(
        functools.partial(kernel, n_seq, n_head, pair),
        out_shape=jax.ShapeDtypeStruct((2, channels, tokens), jnp.float32),
        in_specs=[hbm] * 14,
        out_specs=vmem,
        scratch_shapes=[
            pltpu.VMEM(new_kv.shape, jnp.bfloat16),
            pltpu.VMEM(cache_kv.shape, jnp.bfloat16),
            pltpu.VMEM((1, slots), jnp.int32),
            pltpu.VMEM((1, 1), jnp.int32),
            pltpu.VMEM(hidden.shape, jnp.bfloat16),
            pltpu.VMEM((share // 128, 128), jnp.float32),
            pltpu.VMEM((share // 128, 128), jnp.float32),
            pltpu.VMEM((channels, share), jnp.float32),
            pltpu.VMEM((channels, tokens), jnp.float32),
            pltpu.VMEM((channels, tokens), jnp.float32),
            pltpu.VMEM((1, 1), jnp.float32),
            pltpu.VMEM((heads, groups, slots, HD), jnp.bfloat16),
            pltpu.VMEM((heads, pair, 2, tokens, HD), jnp.bfloat16),
            pltpu.VMEM(text_kv.shape, jnp.bfloat16),
            pltpu.VMEM((n_head, width, share), jnp.bfloat16),
            pltpu.VMEM((heads, groups, slots, HD), jnp.bfloat16),
            pltpu.VMEM((heads, groups, slots, HD), jnp.bfloat16),
            pltpu.VMEM((heads, groups, 8, slots), jnp.float32),
            pltpu.VMEM((heads, groups, 8, slots), jnp.float32),
            pltpu.VMEM((n_head, slots, share), jnp.bfloat16),
            pltpu.VMEM((n_head, slots, share), jnp.bfloat16),
            pltpu.VMEM((n_head, slots + 8, 128), jnp.float32),
            dma((12 + heads + n_head,)),
            dma((heads,)),
            dma((heads,)),
            dma((heads, groups)),
            dma((heads, groups)),
            dma((heads, groups)),
            dma((heads, groups)),
            dma((heads, groups)),
            dma((heads, groups)),
            dma((n_head,)),
            dma((n_head,)),
            dma((n_head,)),
            dma((n_head,)),
        ],
        compiler_params=pltpu.CompilerParams(
            collective_id=0, has_side_effects=True, vmem_limit_bytes=60 * 1024 * 1024
        ),
        cost_estimate=pl.CostEstimate(
            flops=flops, bytes_accessed=2 * w_out.size, transcendentals=0
        ),
    )(
        query,
        new_kv,
        cache_kv,
        text_kv,
        active.reshape(1, slots),
        counts.reshape(1, 1),
        hidden,
        w_out,
        mod_shift.reshape(share // 128, 128),
        mod_scale.reshape(share // 128, 128),
        w_final.T,
        latent.T,
        cached_velocity.T,
        step_size.reshape(1, 1),
    )
    return (result[0].T, result[1].T)


def solution(mesh):
    in_specs = (
        P("seq", "head"),
        P(None, "seq", "head"),
        P(None, "seq", "head"),
        P(None, None, "head"),
        P("seq"),
        P("seq"),
        P("seq", "head"),
        P("head", None),
        P("head"),
        P("head"),
        P("head", None),
        P("seq", None),
        P("seq", None),
        P(),
    )
    out_specs = (P("seq", None), P("seq", None))
    return jax.shard_map(
        functools.partial(on_device, mesh.shape["seq"], mesh.shape["head"]),
        mesh=mesh,
        in_specs=in_specs,
        out_specs=out_specs,
        check_vma=False,
    )
```
